1024 devices in a mesh: dp: 8 (over x, core), expert: 16 (over z_lo), tensor: 8 (over y, z_hi).
Axes of the slice: x: 4, y: 4, z: 32 (z_hi: 2, z_lo: 16; z = z_hi * 16 + z_lo), core: 2. Of those that a mesh axis runs over, the one named last changes fastest.
Arguments:
- hidden: bfloat16 [8, 16, 768, 1536], P('dp', 'expert'), may hold values from -6 to 6
- out_grad: bfloat16 [8, 16, 768, 4096], P('dp', 'expert', None, 'tensor'), may hold values from -0.119628906 to 0.119628906
- block_list: int32 [8, 16, 6], P('dp', 'expert'), may hold values from 0 to 5, each once within a row
- block_count: int32 [8, 16], P('dp', 'expert'), may hold values from 1 to 6, as said below
- first_moment: float32 [1536, 16, 4096], P('dp', 'expert', 'tensor'), may hold values from -3 to 3
- second_moment: float32 [1536, 16, 4096], P('dp', 'expert', 'tensor'), may hold values from 0.05 to 2
- changed: int32 [8, 16, 8, 12], P('dp', 'expert', 'tensor'), may hold values 0 or 1
- placement: int32 [8, 16, 8, 12, 2], P('dp', 'expert', 'tensor'), may hold values from 0 to 15, all different within a row; in each aligned block of 12 rows (0 to 11, 12 to 23, ..., all dimensions but the last counted through in order) at most 2 rows name the same one
Outputs:
- first_next: float32 [1536, 16, 4096], P('dp', 'expert', 'tensor')
- second_next: float32 [1536, 16, 4096], P('dp', 'expert', 'tensor')
- rollout_inbox: bfloat16 [8, 16, 8, 16, 2, 16, 512], P('dp', 'expert', 'tensor')
The draws below stay inside these ranges and needn't reach their ends.
Inputs may be any that keep to these rules, and one draw needn't show every extreme that they name: `block_list`: each buffer's list holds each of its 6 blocks once; its first block_count entries are the live blocks. `block_count`: some buffer has all its blocks live. `placement`: the 2 owners of a slice differ; among the slices of one device no owner is named more than 2 times, a bound that some block reaches.
All inputs are finite; a program needn't handle non-finite values. No bound on the sum of `changed` on one device may be relied on, other than what follows from the above.
Results may differ from the reference program's by a relative error of at most 0.0075.
Values may be sent and summed in bfloat16 or wider, within the bound.
A program may use at most 64 MiB of HBM per device.

```python
import math
import jax
import jax.numpy as jnp
import numpy as np
from jax import lax

D = 4096
FF = 1536
BLOCK = 128
BLOCKS_DEV = 6
SLICES_EXP = 12
REPL = 2
TOK = 768
EXPERTS = 16
CAP = 2
N_DP = 8
N_EXPERT = 16
N_TENSOR = 8


def draw_block_count(key, part):
    key = jax.random.fold_in(key, 7)
    first_draw = jax.random.randint(jax.random.fold_in(key, 1), (N_DP, N_EXPERT), 0, BLOCKS_DEV)
    second_draw = jax.random.randint(jax.random.fold_in(key, 2), (N_DP, N_EXPERT), 0, BLOCKS_DEV)
    counts = jnp.minimum(first_draw, second_draw) + 1
    chosen = jax.random.randint(jax.random.fold_in(key, 3), (), 0, N_DP * N_EXPERT)
    flattened = jnp.where(jnp.arange(N_DP * N_EXPERT) == chosen, BLOCKS_DEV, counts.reshape(-1))
    return flattened.reshape(N_DP, N_EXPERT).astype(jnp.int32)


def plant(drawn, own_key, smallest, top_value):
    spot = [jax.random.randint(jax.random.fold_in(own_key, axis), (), 0, length) for axis, length in enumerate(drawn.shape)]
    main_axis = drawn.shape.index(max(drawn.shape))
    next_to = spot[:main_axis] + [(spot[main_axis] + 1) % drawn.shape[main_axis]] + spot[main_axis + 1:]
    return drawn.at[tuple(spot)].set(smallest).at[tuple(next_to)].set(top_value)


def steps_of(own_key, shape, split, smallest, largest):
    def one(dim, shards_of):
        draws = jax.random.uniform(jax.random.fold_in(jax.random.fold_in(own_key, 6), dim), (shards_of,), jnp.float32, smallest / len(split), largest / len(split))
        return jnp.repeat(jnp.exp(draws), shape[dim] // shards_of).reshape((-1,) + (1,) * (len(shape) - dim - 1))

    gain = one(*split[0])
    for cut in split[1:]:
        gain = gain * one(*cut)
    return gain


def routed_block(stream_key, own, number, rows, number_of, top, most, lean):
    ranking = jax.random.permutation(stream_key, number_of)
    crowded, usual = load_shares(number_of, rows * top, most, lean, True), load_shares(number_of, rows * top, most, lean, False)
    places = jnp.arange(number_of)

    def named(lengths, turn):
        used = int((lengths > 0).sum())
        fixed = max(1, used // 4)
        moved = fixed + (places - fixed + turn * (used - fixed)) % max(1, number_of - fixed)
        return jnp.zeros((number_of,), jnp.int32).at[ranking[jnp.where(places < fixed, places, moved)]].set(jnp.asarray(lengths, jnp.int32))

    lengths = jnp.where(number % 4 == 0, named(crowded, number // 4), named(usual, number - number // 4 - 1))
    mixed = jax.random.permutation(jax.random.fold_in(own, 3), number_of)
    giver, taker = mixed[0:number_of // 2 * 2:2], mixed[1:number_of // 2 * 2:2]
    slack = jnp.minimum(lengths[giver] - 1, most - lengths[taker]) // 2
    slack = jnp.where((giver == ranking[0]) | (taker == ranking[0]) | (lengths[taker] == 0), 0, jnp.maximum(slack, 0))
    moved = jax.random.randint(jax.random.fold_in(own, 4), (number_of // 2,), 0, 1 << 20) % (slack + 1)
    lengths = lengths.at[giver].add(-moved).at[taker].add(moved)
    labels = jnp.searchsorted(jnp.cumsum(lengths), jnp.arange(rows * top), side="right").astype(jnp.int32)
    grid = labels.reshape(top, rows).T
    grid = grid[jax.random.permutation(jax.random.fold_in(own, 1), rows)]
    turn = jax.random.randint(jax.random.fold_in(own, 2), (rows, 1), 0, top)
    return jnp.take_along_axis(grid, (jnp.arange(top)[None, :] + turn) % top, axis=1)


def load_shares(count, total, bound, skew, full):
    portions = [(1 << 20) // math.isqrt(standing ** skew) + 1 for standing in range(1, count + 1)]
    largest = bound if full else min(bound, max(-(-total // count), total * portions[0] // sum(portions)))
    least = 1 if total - largest >= count - 1 else 0
    given, spare = [largest] + [least] * (count - 1), total - largest - least * (count - 1)
    while spare > 0:
        candidates = [i for i in range(1, count) if given[i] < largest] or [i for i in range(1, count) if given[i] < bound]
        whole, remaining = sum([portions[i] for i in candidates]), spare
        for i in candidates:
            more = min(bound - given[i], max(1, remaining * portions[i] // whole), spare)
            given[i] = given[i] + more
            spare = spare - more
    return np.array(given)


def scatter_about(key, shape, deviation, bound, shards=(), dtype=jnp.bfloat16):
    values = jax.random.normal(key, shape, jnp.float32) * deviation
    if len(shards) > 0:
        values = steps_of(key, shape, shards, -0.22, 0.18) * values
    return jnp.clip(values, min=-bound, max=bound).astype(dtype)


def setup_inputs(seed: int = 0) -> dict:
    streams_of = jax.random.split(jax.random.key(seed), 9)
    hidden = scatter_about(streams_of[0], (N_DP, N_EXPERT, TOK, FF), 1.0, 6.0, ((0, 8), (1, 16)))
    out_grad = scatter_about(streams_of[1], (N_DP, N_EXPERT, TOK, D), 0.02, 0.119628906, ((0, 8), (1, 16), (3, 8)))
    block_list = jax.vmap(lambda own: jax.random.permutation(own, BLOCKS_DEV))(jax.random.split(streams_of[2], N_DP * N_EXPERT)).reshape((N_DP, N_EXPERT, BLOCKS_DEV)).astype(jnp.int32)
    block_count = draw_block_count(jax.random.fold_in(streams_of[8], 71), 0)
    first_moment = scatter_about(streams_of[4], (FF, EXPERTS, D), 0.5, 3.0, ((0, 8), (1, 16), (2, 8)), jnp.float32)
    second_moment = jnp.clip(jnp.exp(math.log(2.0) - 3.6888794 * jax.random.uniform(streams_of[5], (FF, EXPERTS, D), jnp.float32) ** steps_of(streams_of[5], (FF, EXPERTS, D), ((0, 8), (1, 16), (2, 8)), -0.2, 0.2)), 0.05, 2.0)
    changed = plant((jax.random.randint(streams_of[6], (N_DP, N_EXPERT, N_TENSOR, SLICES_EXP), 0, 4) < 3).astype(jnp.int32), jax.random.fold_in(streams_of[6], 1), 0, 1)
    placement_keys = jax.random.split(jax.random.fold_in(streams_of[7], 1), N_DP * N_EXPERT * N_TENSOR * SLICES_EXP // SLICES_EXP)
    placement_turns = jax.random.permutation(jax.random.fold_in(streams_of[7], 3), N_DP * N_EXPERT * N_TENSOR * SLICES_EXP // SLICES_EXP)
    placement = jax.vmap(lambda own, number: routed_block(jax.random.fold_in(streams_of[7], 2), own, number, SLICES_EXP, N_EXPERT, REPL, CAP, 2))(placement_keys, placement_turns).reshape((N_DP, N_EXPERT, N_TENSOR, SLICES_EXP, REPL))
    return dict(hidden=hidden, out_grad=out_grad, block_list=block_list, block_count=block_count, first_moment=first_moment, second_moment=second_moment, changed=changed, placement=placement)


def slot_targets(owners, capacity):
    entries = owners.shape[-2] * owners.shape[-1]
    flattened = owners.reshape(owners.shape[:-2] + (entries,))
    matching = flattened[..., :, None] == flattened[..., None, :]
    earlier = jnp.arange(entries)[None, :] < jnp.arange(entries)[:, None]
    slot_rank = lax.optimization_barrier(jnp.sum((matching & earlier).astype(jnp.int32), axis=-1))
    return (flattened * capacity + slot_rank).reshape(owners.shape)

def reference(hidden, out_grad, block_list, block_count, first_moment, second_moment, changed, placement):
    hidden_rows = FF // N_DP
    feature_cols = D // N_TENSOR
    slice_rows = hidden_rows // SLICES_EXP
    blocks = jnp.arange(BLOCKS_DEV)
    listed = blocks[None, None, :] < block_count[:, :, None]
    live_block = jnp.any((block_list[..., :, None] == blocks) & listed[..., :, None], axis=-2)
    token_live = jnp.repeat(live_block, BLOCK, axis=-1).astype(jnp.float32)
    targets = slot_targets(placement, CAP)
    choose = lax.optimization_barrier(jnp.sum((jnp.arange(N_EXPERT * CAP)[:, None, None] == targets[..., None, :, :]).astype(jnp.int32), axis=-1))
    choose = choose.astype(jnp.float32)

    def one_expert(inputs):
        acts, cotan, live, moment_one, moment_two, keep, select = inputs
        gradient = jnp.zeros((FF, D), jnp.float32)
        for data_idx in range(N_DP):
            masked = acts[data_idx].astype(jnp.float32) * live[data_idx][:, None]
            gradient = gradient + jnp.dot(masked.T, cotan[data_idx].astype(jnp.float32), precision=lax.Precision.HIGHEST, preferred_element_type=jnp.float32)
        keep_rows = jnp.transpose(keep, (0, 2, 1))[:, :, None, :, None] > 0
        keep_full = jnp.broadcast_to(keep_rows, (N_DP, SLICES_EXP, slice_rows, N_TENSOR, feature_cols)).reshape(FF, D)
        m_next = 0.9 * moment_one + 0.1 * gradient
        v_next = 0.95 * moment_two + 0.05 * gradient * gradient
        update = m_next / (1.0 - 0.9 ** 50.0) / (jnp.sqrt(v_next / (1.0 - 0.95 ** 50.0)) + 1e-08)
        new_one = jnp.where(keep_full, m_next, moment_one)
        new_two = jnp.where(keep_full, v_next, moment_two)
        update = jnp.where(keep_full, update, 0.0).astype(jnp.bfloat16)
        pieces = update.reshape(N_DP, SLICES_EXP, slice_rows, N_TENSOR, feature_cols)
        pieces = jnp.transpose(pieces, (0, 3, 1, 2, 4)).reshape(N_DP, N_TENSOR, SLICES_EXP, slice_rows * feature_cols)
        outgoing = jnp.einsum('atns,atsk->atnk', select, pieces.astype(jnp.float32)).astype(jnp.bfloat16)
        outgoing = outgoing.reshape(N_DP, N_TENSOR, N_EXPERT, CAP, slice_rows, feature_cols)
        return (new_one, new_two, outgoing)
    inputs = (jnp.transpose(hidden, (1, 0, 2, 3)), jnp.transpose(out_grad, (1, 0, 2, 3)), jnp.transpose(token_live, (1, 0, 2)), jnp.transpose(first_moment, (1, 0, 2)), jnp.transpose(second_moment, (1, 0, 2)), jnp.transpose(changed, (1, 0, 2, 3)), jnp.transpose(choose, (1, 0, 2, 3, 4)))
    new_one, new_two, outgoing = lax.map(one_expert, inputs)
    first_next = jnp.transpose(new_one, (1, 0, 2))
    second_next = jnp.transpose(new_two, (1, 0, 2))
    rollout_inbox = jnp.transpose(outgoing, (1, 3, 2, 0, 4, 5, 6))
    return (first_next, second_next, rollout_inbox)
```

```python
import functools

import jax
import jax.numpy as jnp
from jax import lax
from jax.experimental import pallas as pl
from jax.experimental.pallas import tpu as pltpu
from jax.sharding import PartitionSpec as P

MESH = pl.DeviceIdType.MESH
BLOCK = 128
LANES = 128
SLOTS = 2
STRIDE = 5

beta_one = 0.9
beta_two = 0.95
adam_eps = 1e-08
step_number = 50.0


def kernel(
    n_dp,
    n_exp,
    slices,
    hidden,
    out_grad,
    block_list,
    block_count,
    first,
    second,
    changed,
    placement,
    first_out,
    second_out,
    inbox,
    h_buf,
    g_buf,
    ht_buf,
    m_buf,
    v_buf,
    keep_buf,
    part,
    part_in,
    upd,
    pack,
    pack_in,
    idx_vec,
    idx,
    load_sem,
    idx_sem,
    rs_send,
    rs_recv,
    z_send,
    z_recv,
    near,
    relay_left,
    relay_right,
):
    dp = lax.axis_index("dp")
    me = lax.axis_index("expert")
    tokens, hidden_all = h_buf.shape
    rows = hidden_all // n_dp
    slice_rows = rows // slices
    chunks = g_buf.shape[1] // LANES
    blocks = tokens // BLOCK

    barrier = pltpu.get_barrier_semaphore()
    for off in range(1, n_dp):
        pl.semaphore_signal(
            barrier, inc=1, device_id={"dp": lax.rem(dp + off, n_dp)}, device_id_type=MESH
        )
    for off in range(1, STRIDE + 1):

        @pl.when(me + off < n_exp)
        def _():
            pl.semaphore_signal(
                barrier, inc=1, device_id={"expert": me + off}, device_id_type=MESH
            )

    groups = hidden_all // 512
    loads = [pltpu.make_async_copy(out_grad.at[0, 0], g_buf, load_sem.at[0])]
    for i in range(groups):
        cols = pl.ds(i * 512, 512)
        loads.append(
            pltpu.make_async_copy(hidden.at[0, 0, :, cols], h_buf.at[:, cols], load_sem.at[1 + i])
        )
    loads.append(pltpu.make_async_copy(first, m_buf, load_sem.at[1 + groups]))
    loads.append(pltpu.make_async_copy(second, v_buf, load_sem.at[2 + groups]))
    for cp in loads:
        cp.start()

    lane = lax.broadcasted_iota(jnp.int32, (8, LANES), 1)
    owner_of = lane // SLOTS
    slot_of = lane - owner_of * SLOTS
    count = jnp.zeros((8, LANES), jnp.int32)
    table = jnp.full((8, LANES), slices, jnp.int32)
    for s in range(slices):
        value = jnp.where(changed[0, 0, 0, s] > 0, s, slices)
        for k in range(2):
            hit = owner_of == placement[0, 0, 0, k, s]
            table = jnp.where(hit & (count == slot_of), value, table)
            count = count + hit.astype(jnp.int32)
    idx_vec[...] = table
    idx_copy = pltpu.make_async_copy(idx_vec, idx, idx_sem)
    idx_copy.start()
    for s in range(slices):
        keep_buf[pl.ds(s * slice_rows, slice_rows), :] = jnp.full(
            (slice_rows, LANES), changed[0, 0, 0, s], jnp.int32
        )
    upd[slices] = jnp.zeros(upd.shape[1:], upd.dtype)

    loads[0].wait()
    for b in range(blocks):
        live = jnp.int32(0)
        for j in range(blocks):
            hit = (block_list[0, 0, j] == b) & (block_count[0, 0] > j)
            live = live | hit.astype(jnp.int32)
        at = pl.ds(b * BLOCK, BLOCK)
        block = g_buf[at, :]
        g_buf[at, :] = jnp.where(live > 0, block, jnp.zeros_like(block))
    for i in range(groups):
        loads[1 + i].wait()
        for j in range(512 // LANES):
            at = i * 512 + j * LANES
            ht_buf[pl.ds(at, LANES), :] = h_buf[:, pl.ds(at, LANES)].T

    def reduce_copy(c, peer, slot):
        return pltpu.make_async_remote_copy(
            src_ref=part.at[c, peer],
            dst_ref=part_in.at[c, slot],
            send_sem=rs_send.at[c, peer],
            recv_sem=rs_recv.at[c, slot],
            device_id={"dp": peer},
            device_id_type=MESH,
        )

    for c in range(chunks):
        for d in range(n_dp):
            prod = jnp.dot(
                ht_buf[pl.ds(d * rows, rows), :],
                g_buf[:, pl.ds(c * LANES, LANES)],
                preferred_element_type=jnp.float32,
            )
            part[c, d] = prod.astype(part.dtype)
        if c == 0:
            pl.semaphore_wait(barrier, n_dp - 1 + jnp.minimum(me, STRIDE))
            for off in range(1, STRIDE + 1):

                @pl.when(me - off >= 0)
                def _():
                    pl.semaphore_signal(
                        near, inc=1, device_id={"expert": me - off}, device_id_type=MESH
                    )
        for off in range(1, n_dp):
            reduce_copy(c, lax.rem(dp + off, n_dp), dp).start()

    loads[1 + groups].wait()
    loads[2 + groups].wait()
    idx_copy.wait()

    def tell(sem, peer):
        pl.semaphore_signal(sem, inc=1, device_id={"expert": peer}, device_id_type=MESH)

    @pl.when(me + 1 < n_exp)
    def _():
        pl.semaphore_wait(near, jnp.minimum(n_exp - 1 - me, STRIDE))

    @pl.when((me + STRIDE < n_exp) & (me > 0))
    def _():
        tell(relay_left.at[0], me + STRIDE)

    @pl.when((me - STRIDE >= 0) & (me + 1 < n_exp))
    def _():
        tell(relay_right.at[0], me - STRIDE)

    hops = -(-(n_exp - 1) // STRIDE) - 1

    def learn(sems, reach, onward, far_enough):
        for h in range(hops):

            @pl.when(reach > (h + 1) * STRIDE)
            def _():
                pl.semaphore_wait(sems.at[h], 1)

            if h + 1 < hops:

                @pl.when(far_enough & (reach > (h + 1) * STRIDE))
                def _():
                    tell(sems.at[h + 1], onward)

    def route_copy(c, peer, slot):
        return pltpu.make_async_remote_copy(
            src_ref=pack.at[c, peer],
            dst_ref=pack_in.at[c, slot],
            send_sem=z_send.at[c, peer],
            recv_sem=z_recv.at[c, slot],
            device_id={"expert": peer},
            device_id_type=MESH,
        )

    corr_one = 1.0 - beta_one**step_number
    corr_two = 1.0 - beta_two**step_number
    for c in range(chunks):
        total = part[c, dp].astype(jnp.float32)
        for off in range(1, n_dp):
            peer = lax.rem(dp + off, n_dp)
            reduce_copy(c, peer, peer).wait_recv()
            total = total + part_in[c, peer].astype(jnp.float32)
        at = pl.ds(c, rows, stride=chunks)
        m_old = m_buf[at, :]
        v_old = v_buf[at, :]
        keep = keep_buf[...] > 0
        m_next = beta_one * m_old + (1.0 - beta_one) * total
        v_next = beta_two * v_old + (1.0 - beta_two) * total * total
        update = m_next / corr_one / (jnp.sqrt(v_next / corr_two) + adam_eps)
        first_out[at, :] = jnp.where(keep, m_next, m_old)
        second_out[at, :] = jnp.where(keep, v_next, v_old)
        upd[pl.ds(0, slices)] = update.astype(upd.dtype).reshape(slices, slice_rows, LANES)
        for n in range(n_exp * SLOTS):
            pack[c, n // SLOTS, n % SLOTS] = upd[idx[0, n]]
        if c == 0:
            learn(relay_left, me, me + STRIDE, me + STRIDE < n_exp)

        @pl.loop(0, n_exp - 1)
        def _(i):
            @pl.when(i < me)
            def _():
                route_copy(c, i, me).start()

        @pl.loop(1, STRIDE + 1)
        def _(off):
            @pl.when(me + off < n_exp)
            def _():
                route_copy(c, me + off, me).start()

        if c == 0:
            learn(relay_right, n_exp - 1 - me, me - STRIDE, me - STRIDE >= 0)

        @pl.loop(STRIDE + 1, n_exp)
        def _(off):
            @pl.when(me + off < n_exp)
            def _():
                route_copy(c, me + off, me).start()

    for c in range(chunks):
        cols = pl.ds(c * LANES, LANES)
        inbox[me, :, :, cols] = pack[c, me]

        @pl.loop(1, n_exp)
        def _(off):
            peer = lax.rem(me + off, n_exp)
            route_copy(c, peer, peer).wait_recv()
            inbox[peer, :, :, cols] = pack_in[c, peer]

    for c in range(chunks):
        for off in range(1, n_dp):
            reduce_copy(c, lax.rem(dp + off, n_dp), dp).wait_send()

        @pl.loop(1, n_exp)
        def _(off):
            route_copy(c, lax.rem(me + off, n_exp), me).wait_send()


def on_device(
    hidden, out_grad, block_list, block_count, first_moment, second_moment, changed, placement
):
    n_dp = lax.axis_size("dp")
    n_exp = lax.axis_size("expert")
    tokens, hidden_all = hidden.shape[2:]
    features = out_grad.shape[3]
    slices = changed.shape[3]
    rows = first_moment.shape[0]
    slice_rows = rows // slices
    chunks = features // LANES
    flat = (rows * chunks, LANES)
    f32, bf16 = jnp.float32, jnp.bfloat16
    any_spec = pl.BlockSpec(memory_space=pltpu.HBM)
    smem = pl.BlockSpec(memory_space=pltpu.SMEM)
    vmem = pl.BlockSpec(memory_space=pltpu.VMEM)
    dma = pltpu.SemaphoreType.DMA
    regular = pltpu.SemaphoreType.REGULAR
    first_next, second_next, inbox = pl.pallas_call(
        functools.partial(kernel, n_dp, n_exp, slices),
        out_shape=(
            jax.ShapeDtypeStruct(flat, f32),
            jax.ShapeDtypeStruct(flat, f32),
            jax.ShapeDtypeStruct((n_exp, SLOTS, slice_rows, features), bf16),
        ),
        in_specs=[any_spec, any_spec, smem, smem, any_spec, any_spec, smem, smem],
        out_specs=(vmem, vmem, vmem),
        scratch_shapes=[
            pltpu.VMEM((tokens, hidden_all), bf16),
            pltpu.VMEM((tokens, features), bf16),
            pltpu.VMEM((hidden_all, tokens), bf16),
            pltpu.VMEM(flat, f32),
            pltpu.VMEM(flat, f32),
            pltpu.VMEM((rows, LANES), jnp.int32),
            pltpu.VMEM((chunks, n_dp, rows, LANES), bf16),
            pltpu.VMEM((chunks, n_dp, rows, LANES), bf16),
            pltpu.VMEM((slices + 1, slice_rows, LANES), bf16),
            pltpu.VMEM((chunks, n_exp, SLOTS, slice_rows, LANES), bf16),
            pltpu.VMEM((chunks, n_exp, SLOTS, slice_rows, LANES), bf16),
            pltpu.VMEM((8, LANES), jnp.int32),
            pltpu.SMEM((8, LANES), jnp.int32),
            dma((3 + hidden_all // 512,)),
            dma(()),
            dma((chunks, n_dp)),
            dma((chunks, n_dp)),
            dma((chunks, n_exp)),
            dma((chunks, n_exp)),
            regular(()),
            regular((4,)),
            regular((4,)),
        ],
        compiler_params=pltpu.CompilerParams(
            collective_id=0, has_side_effects=True, vmem_limit_bytes=60 << 20
        ),
    )(
        hidden,
        out_grad,
        block_list,
        block_count,
        first_moment.reshape(flat),
        second_moment.reshape(flat),
        changed,
        jnp.swapaxes(placement, 3, 4),
    )
    shape = first_moment.shape
    return (
        first_next.reshape(shape),
        second_next.reshape(shape),
        inbox[None, None, None],
    )


def solution(mesh):
    return jax.shard_map(
        on_device,
        mesh=mesh,
        in_specs=(
            P("dp", "expert", None, None),
            P("dp", "expert", None, "tensor"),
            P("dp", "expert", None),
            P("dp", "expert"),
            P("dp", "expert", "tensor"),
            P("dp", "expert", "tensor"),
            P("dp", "expert", "tensor", None),
            P("dp", "expert", "tensor", None, None),
        ),
        out_specs=(
            P("dp", "expert", "tensor"),
            P("dp", "expert", "tensor"),
            P("dp", "expert", "tensor", None, None, None, None),
        ),
        check_vma=False,
    )
```

```python
import functools

import jax
import jax.numpy as jnp
from jax import lax
from jax.experimental import pallas as pl
from jax.experimental.pallas import tpu as pltpu
from jax.sharding import PartitionSpec as P

MESH = pl.DeviceIdType.MESH
BLOCK = 128
LANES = 128
SLOTS = 2
STRIDE = 5

beta_one = 0.9
beta_two = 0.95
adam_eps = 1e-08
step_number = 50.0


def kernel(
    n_dp,
    n_exp,
    slices,
    hidden,
    out_grad,
    block_list_hbm,
    block_count,
    first,
    second,
    changed_hbm,
    placement_hbm,
    first_out,
    second_out,
    pack_in,
    block_list,
    changed,
    placement,
    h_buf,
    g_buf,
    ht_buf,
    m_buf,
    v_buf,
    keep_buf,
    part,
    part_in,
    upd,
    pack,
    idx_vec,
    idx,
    load_sem,
    small_sem,
    idx_sem,
    rs_send,
    rs_recv,
    z_send,
    z_recv,
    near,
    relay_left,
    relay_right,
):
    dp = lax.axis_index("dp")
    me = lax.axis_index("expert")
    tokens, hidden_all = h_buf.shape
    rows = hidden_all // n_dp
    slice_rows = rows // slices
    chunks = g_buf.shape[1] // LANES
    blocks = tokens // BLOCK

    barrier = pltpu.get_barrier_semaphore()
    for off in range(1, n_dp):
        pl.semaphore_signal(
            barrier, inc=1, device_id={"dp": lax.rem(dp + off, n_dp)}, device_id_type=MESH
        )
    for off in range(1, STRIDE + 1):

        @pl.when(me + off < n_exp)
        def _():
            pl.semaphore_signal(
                barrier, inc=1, device_id={"expert": me + off}, device_id_type=MESH
            )

    small = [
        pltpu.make_async_copy(src, dst, small_sem.at[i])
        for i, (src, dst) in enumerate(
            (
                (changed_hbm, changed),
                (placement_hbm, placement),
                (block_list_hbm, block_list),
            )
        )
    ]
    for cp in small:
        cp.start()
    groups = hidden_all // 512
    loads = [pltpu.make_async_copy(out_grad.at[0, 0], g_buf, load_sem.at[0])]
    for i in range(groups):
        cols = pl.ds(i * 512, 512)
        loads.append(
            pltpu.make_async_copy(hidden.at[0, 0, :, cols], h_buf.at[:, cols], load_sem.at[1 + i])
        )
    loads.append(pltpu.make_async_copy(first, m_buf, load_sem.at[1 + groups]))
    loads.append(pltpu.make_async_copy(second, v_buf, load_sem.at[2 + groups]))
    for cp in loads:
        cp.start()

    for cp in small:
        cp.wait()
    lane = lax.broadcasted_iota(jnp.int32, (8, LANES), 1)
    owner_of = lane // SLOTS
    slot_of = lane - owner_of * SLOTS
    count = jnp.zeros((8, LANES), jnp.int32)
    table = jnp.full((8, LANES), slices, jnp.int32)
    for s in range(slices):
        value = jnp.where(changed[0, 0, 0, s] > 0, s, slices)
        for k in range(2):
            hit = owner_of == placement[0, 0, 0, k, s]
            table = jnp.where(hit & (count == slot_of), value, table)
            count = count + hit.astype(jnp.int32)
    idx_vec[...] = table
    idx_copy = pltpu.make_async_copy(idx_vec, idx, idx_sem)
    idx_copy.start()
    for s in range(slices):
        keep_buf[pl.ds(s * slice_rows, slice_rows), :] = jnp.full(
            (slice_rows, LANES), changed[0, 0, 0, s], jnp.int32
        )
    upd[slices] = jnp.zeros(upd.shape[1:], upd.dtype)

    loads[0].wait()
    for b in range(blocks):
        live = jnp.int32(0)
        for j in range(blocks):
            hit = (block_list[0, 0, j] == b) & (block_count[0, 0] > j)
            live = live | hit.astype(jnp.int32)
        at = pl.ds(b * BLOCK, BLOCK)
        block = g_buf[at, :]
        g_buf[at, :] = jnp.where(live > 0, block, jnp.zeros_like(block))
    for i in range(groups):
        loads[1 + i].wait()
        for j in range(512 // LANES):
            at = i * 512 + j * LANES
            ht_buf[pl.ds(at, LANES), :] = h_buf[:, pl.ds(at, LANES)].T

    pl.semaphore_wait(barrier, n_dp - 1 + jnp.minimum(me, STRIDE))
    for off in range(1, STRIDE + 1):

        @pl.when(me - off >= 0)
        def _():
            pl.semaphore_signal(
                near, inc=1, device_id={"expert": me - off}, device_id_type=MESH
            )

    def reduce_copy(c, peer, slot):
        return pltpu.make_async_remote_copy(
            src_ref=part.at[c, peer],
            dst_ref=part_in.at[c, slot],
            send_sem=rs_send.at[c, peer],
            recv_sem=rs_recv.at[c, slot],
            device_id={"dp": peer},
            device_id_type=MESH,
        )

    for c in range(chunks):
        for d in range(n_dp):
            prod = jnp.dot(
                ht_buf[pl.ds(d * rows, rows), :],
                g_buf[:, pl.ds(c * LANES, LANES)],
                preferred_element_type=jnp.float32,
            )
            part[c, d] = prod.astype(part.dtype)
        for off in range(1, n_dp):
            reduce_copy(c, lax.rem(dp + off, n_dp), dp).start()

    loads[1 + groups].wait()
    loads[2 + groups].wait()
    idx_copy.wait()

    def tell(sem, peer):
        pl.semaphore_signal(sem, inc=1, device_id={"expert": peer}, device_id_type=MESH)

    @pl.when(me + 1 < n_exp)
    def _():
        pl.semaphore_wait(near, jnp.minimum(n_exp - 1 - me, STRIDE))

    @pl.when((me + STRIDE < n_exp) & (me > 0))
    def _():
        tell(relay_left.at[0], me + STRIDE)

    @pl.when((me - STRIDE >= 0) & (me + 1 < n_exp))
    def _():
        tell(relay_right.at[0], me - STRIDE)

    hops = -(-(n_exp - 1) // STRIDE) - 1

    def learn(sems, reach, onward, far_enough):
        for h in range(hops):

            @pl.when(reach > (h + 1) * STRIDE)
            def _():
                pl.semaphore_wait(sems.at[h], 1)

            if h + 1 < hops:

                @pl.when(far_enough & (reach > (h + 1) * STRIDE))
                def _():
                    tell(sems.at[h + 1], onward)

    phases = ((0, 1), (1, 1), (2, chunks - 2))

    def route_copy(p, peer, slot):
        at = pl.ds(*phases[p])
        return pltpu.make_async_remote_copy(
            src_ref=pack.at[peer, at],
            dst_ref=pack_in.at[slot, at],
            send_sem=z_send.at[p, peer],
            recv_sem=z_recv.at[p, slot],
            device_id={"expert": peer},
            device_id_type=MESH,
        )

    corr_one = 1.0 - beta_one**step_number
    corr_two = 1.0 - beta_two**step_number
    for c in range(chunks):
        total = part[c, dp].astype(jnp.float32)
        for off in range(1, n_dp):
            peer = lax.rem(dp + off, n_dp)
            reduce_copy(c, peer, peer).wait_recv()
            total = total + part_in[c, peer].astype(jnp.float32)
        at = pl.ds(c, rows, stride=chunks)
        m_old = m_buf[at, :]
        v_old = v_buf[at, :]
        keep = keep_buf[...] > 0
        m_next = beta_one * m_old + (1.0 - beta_one) * total
        v_next = beta_two * v_old + (1.0 - beta_two) * total * total
        update = m_next / corr_one / (jnp.sqrt(v_next / corr_two) + adam_eps)
        first_out[at, :] = jnp.where(keep, m_next, m_old)
        second_out[at, :] = jnp.where(keep, v_next, v_old)
        upd[pl.ds(0, slices)] = update.astype(upd.dtype).reshape(slices, slice_rows, LANES)
        for n in range(n_exp * SLOTS):
            pack[n // SLOTS, c, n % SLOTS] = upd[idx[0, n]]
        if c == 0:
            learn(relay_left, me, me + STRIDE, me + STRIDE < n_exp)
        done = [p for p, (start, size) in enumerate(phases) if start + size == c + 1]
        if not done:
            continue
        p = done[0]

        @pl.loop(0, n_exp - 1)
        def _(i):
            @pl.when(i < me)
            def _():
                route_copy(p, i, me).start()

        @pl.loop(1, STRIDE + 1)
        def _(off):
            @pl.when(me + off < n_exp)
            def _():
                route_copy(p, me + off, me).start()

        if c == 0:
            learn(relay_right, n_exp - 1 - me, me - STRIDE, me - STRIDE >= 0)

        @pl.loop(STRIDE + 1, n_exp)
        def _(off):
            @pl.when(me + off < n_exp)
            def _():
                route_copy(p, me + off, me).start()

    pack_in[me] = pack[me]
    for c in range(chunks):
        for off in range(1, n_dp):
            reduce_copy(c, lax.rem(dp + off, n_dp), dp).wait_send()
    for p in range(len(phases)):

        @pl.loop(1, n_exp)
        def _(off):
            peer = lax.rem(me + off, n_exp)
            route_copy(p, peer, me).wait_send()
            route_copy(p, peer, peer).wait_recv()


def store_kernel(first, second, pack, first_out, second_out, inbox, sem):
    chunks = pack.shape[1]
    copies = [
        pltpu.make_async_copy(first, first_out, sem.at[0]),
        pltpu.make_async_copy(second, second_out, sem.at[1]),
    ]
    for c in range(chunks):
        copies.append(
            pltpu.make_async_copy(
                pack.at[:, c], inbox.at[:, :, :, pl.ds(c * LANES, LANES)], sem.at[2 + c]
            )
        )
    for cp in copies:
        cp.start()
    for cp in copies:
        cp.wait()


def in_hbm(x):
    return pltpu.with_memory_space_constraint(x, pltpu.HBM)


def on_device(
    hidden, out_grad, block_list, block_count, first_moment, second_moment, changed, placement
):
    n_dp = lax.axis_size("dp")
    n_exp = lax.axis_size("expert")
    tokens, hidden_all = hidden.shape[2:]
    features = out_grad.shape[3]
    slices = changed.shape[3]
    rows = first_moment.shape[0]
    slice_rows = rows // slices
    chunks = features // LANES
    flat = (rows * chunks, LANES)
    f32, bf16 = jnp.float32, jnp.bfloat16
    any_spec = pl.BlockSpec(memory_space=pltpu.HBM)
    vmem = pl.BlockSpec(memory_space=pltpu.VMEM)
    dma = pltpu.SemaphoreType.DMA
    regular = pltpu.SemaphoreType.REGULAR
    swapped = jnp.swapaxes(placement, 3, 4)
    results = pl.pallas_call(
        functools.partial(kernel, n_dp, n_exp, slices),
        out_shape=(
            pltpu.VMEM(flat, f32),
            pltpu.VMEM(flat, f32),
            pltpu.VMEM((n_exp, chunks, SLOTS, slice_rows, LANES), bf16),
        ),
        in_specs=[any_spec] * 3 + [pl.BlockSpec(memory_space=pltpu.SMEM)] + [any_spec] * 4,
        out_specs=(vmem, vmem, vmem),
        scratch_shapes=[
            pltpu.SMEM(block_list.shape, jnp.int32),
            pltpu.SMEM(changed.shape, jnp.int32),
            pltpu.SMEM(swapped.shape, jnp.int32),
            pltpu.VMEM((tokens, hidden_all), bf16),
            pltpu.VMEM((tokens, features), bf16),
            pltpu.VMEM((hidden_all, tokens), bf16),
            pltpu.VMEM(flat, f32),
            pltpu.VMEM(flat, f32),
            pltpu.VMEM((rows, LANES), jnp.int32),
            pltpu.VMEM((chunks, n_dp, rows, LANES), bf16),
            pltpu.VMEM((chunks, n_dp, rows, LANES), bf16),
            pltpu.VMEM((slices + 1, slice_rows, LANES), bf16),
            pltpu.VMEM((n_exp, chunks, SLOTS, slice_rows, LANES), bf16),
            pltpu.VMEM((8, LANES), jnp.int32),
            pltpu.SMEM((8, LANES), jnp.int32),
            dma((3 + hidden_all // 512,)),
            dma((3,)),
            dma(()),
            dma((chunks, n_dp)),
            dma((chunks, n_dp)),
            dma((3, n_exp)),
            dma((3, n_exp)),
            regular(()),
            regular((4,)),
            regular((4,)),
        ],
        compiler_params=pltpu.CompilerParams(
            collective_id=0, has_side_effects=True, vmem_limit_bytes=32 << 20
        ),
    )(
        in_hbm(hidden),
        in_hbm(out_grad),
        in_hbm(block_list),
        block_count,
        in_hbm(first_moment.reshape(flat)),
        in_hbm(second_moment.reshape(flat)),
        in_hbm(changed),
        in_hbm(swapped),
    )
    first_next, second_next, inbox = pl.pallas_call(
        store_kernel,
        out_shape=(
            jax.ShapeDtypeStruct(flat, f32),
            jax.ShapeDtypeStruct(flat, f32),
            jax.ShapeDtypeStruct((n_exp, SLOTS, slice_rows, features), bf16),
        ),
        in_specs=[vmem] * 3,
        out_specs=(any_spec,) * 3,
        scratch_shapes=[dma((2 + chunks,))],
    )(*(pltpu.with_memory_space_constraint(x, pltpu.VMEM) for x in results))
    shape = first_moment.shape
    return (
        first_next.reshape(shape),
        second_next.reshape(shape),
        inbox[None, None, None],
    )


def solution(mesh):
    return jax.shard_map(
        on_device,
        mesh=mesh,
        in_specs=(
            P("dp", "expert", None, None),
            P("dp", "expert", None, "tensor"),
            P("dp", "expert", None),
            P("dp", "expert"),
            P("dp", "expert", "tensor"),
            P("dp", "expert", "tensor"),
            P("dp", "expert", "tensor", None),
            P("dp", "expert", "tensor", None, None),
        ),
        out_specs=(
            P("dp", "expert", "tensor"),
            P("dp", "expert", "tensor"),
            P("dp", "expert", "tensor", None, None, None, None),
        ),
        check_vma=False,
    )
```

```python
import functools

import jax
import jax.numpy as jnp
from jax import lax
from jax.experimental import pallas as pl
from jax.experimental.pallas import tpu as pltpu
from jax.sharding import PartitionSpec as P

MESH = pl.DeviceIdType.MESH
BLOCK = 128
LANES = 128
SLOTS = 2

beta_one = 0.9
beta_two = 0.95
adam_eps = 1e-08
step_number = 50.0


def kernel(
    n_dp,
    n_exp,
    slices,
    hidden,
    out_grad,
    block_list_hbm,
    block_count,
    first,
    second,
    changed_hbm,
    placement_hbm,
    first_out,
    second_out,
    pack_in,
    block_list,
    changed,
    placement,
    h_buf,
    g_buf,
    ht_buf,
    m_buf,
    v_buf,
    keep_buf,
    part,
    pair_in,
    part_in,
    upd,
    pack,
    idx_vec,
    idx,
    load_sem,
    small_sem,
    idx_sem,
    pair_send,
    pair_recv,
    rs_send,
    rs_recv,
    z_send,
    z_recv,
    ready,
):
    dp = lax.axis_index("dp")
    me = lax.axis_index("expert")
    pairs = n_dp // 2
    place = dp // 2
    side = dp - 2 * place
    sibling = 2 * place + 1 - side
    tokens, hidden_all = h_buf.shape
    rows = hidden_all // n_dp
    slice_rows = rows // slices
    chunks = g_buf.shape[1] // LANES
    blocks = tokens // BLOCK

    barrier = pltpu.get_barrier_semaphore()
    for peer in [sibling] + [2 * lax.rem(place + off, pairs) + side for off in range(1, pairs)]:
        pl.semaphore_signal(barrier, inc=1, device_id={"dp": peer}, device_id_type=MESH)

    @pl.loop(1, n_exp)
    def _(off):
        @pl.when(me + off < n_exp)
        def _():
            pl.semaphore_signal(
                barrier, inc=1, device_id={"expert": me + off}, device_id_type=MESH
            )

    small = [
        pltpu.make_async_copy(src, dst, small_sem.at[i])
        for i, (src, dst) in enumerate(
            (
                (changed_hbm, changed),
                (placement_hbm, placement),
                (block_list_hbm, block_list),
            )
        )
    ]
    for cp in small:
        cp.start()
    groups = hidden_all // 512
    loads = [pltpu.make_async_copy(out_grad.at[0, 0], g_buf, load_sem.at[0])]
    for i in range(groups):
        cols = pl.ds(i * 512, 512)
        loads.append(
            pltpu.make_async_copy(hidden.at[0, 0, :, cols], h_buf.at[:, cols], load_sem.at[1 + i])
        )
    loads.append(pltpu.make_async_copy(first, m_buf, load_sem.at[1 + groups]))
    loads.append(pltpu.make_async_copy(second, v_buf, load_sem.at[2 + groups]))
    for cp in loads:
        cp.start()

    for cp in small:
        cp.wait()
    loads[0].wait()
    for b in range(blocks):
        live = jnp.int32(0)
        for j in range(blocks):
            hit = (block_list[0, 0, j] == b) & (block_count[0, 0] > j)
            live = live | hit.astype(jnp.int32)
        at = pl.ds(b * BLOCK, BLOCK)
        block = g_buf[at, :]
        g_buf[at, :] = jnp.where(live > 0, block, jnp.zeros_like(block))
    for i in range(groups):
        loads[1 + i].wait()
        for j in range(512 // LANES):
            at = i * 512 + j * LANES
            ht_buf[pl.ds(at, LANES), :] = h_buf[:, pl.ds(at, LANES)].T

    def pair_copy(c):
        return pltpu.make_async_remote_copy(
            src_ref=part.at[c, 1 - side],
            dst_ref=pair_in.at[c],
            send_sem=pair_send.at[c],
            recv_sem=pair_recv.at[c],
            device_id={"dp": sibling},
            device_id_type=MESH,
        )

    def reduce_copy(c, peer, slot):
        return pltpu.make_async_remote_copy(
            src_ref=part.at[c, side, peer],
            dst_ref=part_in.at[c, slot],
            send_sem=rs_send.at[c, peer],
            recv_sem=rs_recv.at[c, slot],
            device_id={"dp": 2 * peer + side},
            device_id_type=MESH,
        )

    def enter():
        pl.semaphore_wait(barrier, pairs + me)

        @pl.loop(1, n_exp)
        def _(off):
            @pl.when(me - off >= 0)
            def _():
                pl.semaphore_signal(
                    ready.at[me], inc=1, device_id={"expert": me - off}, device_id_type=MESH
                )

    def multiply(c):
        width = 2 * LANES
        for d in range(n_dp):
            prod = jnp.dot(
                ht_buf[pl.ds(d * rows, rows), :],
                g_buf[:, pl.ds(c * LANES, width)],
                preferred_element_type=jnp.float32,
            ).astype(part.dtype)
            part[c, d % 2, d // 2] = prod[:, :LANES]
            part[c + 1, d % 2, d // 2] = prod[:, LANES:]
        if c == 0:
            enter()
        pair_copy(c).start()
        pair_copy(c + 1).start()

    def add_pair(c):
        pair_copy(c).wait_recv()
        mine = part[c, side].astype(jnp.float32) + pair_in[c].astype(jnp.float32)
        part[c, side] = mine.astype(part.dtype)
        for off in range(1, pairs):
            reduce_copy(c, lax.rem(place + off, pairs), place).start()

    multiply(0)

    lane = lax.broadcasted_iota(jnp.int32, (8, LANES), 1)
    owner_of = lane // SLOTS
    slot_of = lane - owner_of * SLOTS
    count = jnp.zeros((8, LANES), jnp.int32)
    table = jnp.full((8, LANES), slices, jnp.int32)
    for s in range(slices):
        value = jnp.where(changed[0, 0, 0, s] > 0, s, slices)
        for k in range(2):
            hit = owner_of == placement[0, 0, 0, k, s]
            table = jnp.where(hit & (count == slot_of), value, table)
            count = count + hit.astype(jnp.int32)
    idx_vec[...] = table
    idx_copy = pltpu.make_async_copy(idx_vec, idx, idx_sem)
    idx_copy.start()
    for s in range(slices):
        keep_buf[pl.ds(s * slice_rows, slice_rows), :] = jnp.full(
            (slice_rows, LANES), changed[0, 0, 0, s], jnp.int32
        )
    upd[slices] = jnp.zeros(upd.shape[1:], upd.dtype)

    add_pair(0)
    multiply(2)
    add_pair(1)

    loads[1 + groups].wait()
    loads[2 + groups].wait()
    idx_copy.wait()

    phases = ((0, 1), (1, chunks - 1), (0, chunks))
    middle = 5 * n_exp // 8

    def route_copy(p, peer, slot):
        at = pl.ds(*phases[p])
        return pltpu.make_async_remote_copy(
            src_ref=pack.at[peer, at],
            dst_ref=pack_in.at[slot, at],
            send_sem=z_send.at[p, peer],
            recv_sem=z_recv.at[p, slot],
            device_id={"expert": peer},
            device_id_type=MESH,
        )

    def far_first(low, high, act):
        @pl.loop(0, high - low)
        def _(i):
            act(high - 1 - i)

    def send_left(p):
        def act(off):
            @pl.when(me - off >= 0)
            def _():
                route_copy(p, me - off, me).start()

        return act

    def send_right(p):
        def act(off):
            @pl.when(me + off < n_exp)
            def _():
                if p != 1:
                    pl.semaphore_wait(ready.at[me + off], 1)
                route_copy(p, me + off, me).start()

        return act

    def wait_sent(p):
        def act(off):
            @pl.when(me - off >= 0)
            def _():
                route_copy(p, me - off, me).wait_send()

            @pl.when(me + off < n_exp)
            def _():
                route_copy(p, me + off, me).wait_send()

        return act

    def wait_received(p):
        def act(off):
            @pl.when(me - off >= 0)
            def _():
                route_copy(p, me - off, me - off).wait_recv()

            @pl.when(me + off < n_exp)
            def _():
                route_copy(p, me + off, me + off).wait_recv()

        return act

    corr_one = 1.0 - beta_one**step_number
    corr_two = 1.0 - beta_two**step_number
    for c in range(chunks):
        total = part[c, side, place].astype(jnp.float32)
        for off in range(1, pairs):
            peer = lax.rem(place + off, pairs)
            reduce_copy(c, peer, peer).wait_recv()
            total = total + part_in[c, peer].astype(jnp.float32)
        if c == 0:
            add_pair(2)
            add_pair(3)
        at = pl.ds(c, rows, stride=chunks)
        m_old = m_buf[at, :]
        v_old = v_buf[at, :]
        keep = keep_buf[...] > 0
        m_next = beta_one * m_old + (1.0 - beta_one) * total
        v_next = beta_two * v_old + (1.0 - beta_two) * total * total
        update = m_next / corr_one / (jnp.sqrt(v_next / corr_two) + adam_eps)
        first_out[at, :] = jnp.where(keep, m_next, m_old)
        second_out[at, :] = jnp.where(keep, v_next, v_old)
        upd[pl.ds(0, slices)] = update.astype(upd.dtype).reshape(slices, slice_rows, LANES)
        for n in range(n_exp * SLOTS):
            pack[n // SLOTS, c, n % SLOTS] = upd[idx[0, n]]
        if c == 0:
            far_first(1, middle + 1, send_left(0))
            pl.loop(1, middle + 1)(send_right(0))

    far_first(middle + 1, n_exp, send_left(2))
    far_first(1, middle + 1, send_left(1))
    pl.loop(middle + 1, n_exp)(send_right(2))
    far_first(1, middle + 1, send_right(1))

    pack_in[me] = pack[me]
    for c in range(chunks):
        pair_copy(c).wait_send()
        for off in range(1, pairs):
            reduce_copy(c, lax.rem(place + off, pairs), place).wait_send()
    for p in (0, 1):
        far_first(1, middle + 1, wait_sent(p))
        far_first(1, middle + 1, wait_received(p))
    far_first(middle + 1, n_exp, wait_sent(2))
    far_first(middle + 1, n_exp, wait_received(2))


def store_kernel(first, second, pack, first_out, second_out, inbox, sem):
    chunks = pack.shape[1]
    copies = [
        pltpu.make_async_copy(first, first_out, sem.at[0]),
        pltpu.make_async_copy(second, second_out, sem.at[1]),
    ]
    for c in range(chunks):
        copies.append(
            pltpu.make_async_copy(
                pack.at[:, c], inbox.at[:, :, :, pl.ds(c * LANES, LANES)], sem.at[2 + c]
            )
        )
    for cp in copies:
        cp.start()
    for cp in copies:
        cp.wait()


def in_hbm(x):
    return pltpu.with_memory_space_constraint(x, pltpu.HBM)


def on_device(
    hidden, out_grad, block_list, block_count, first_moment, second_moment, changed, placement
):
    n_dp = lax.axis_size("dp")
    n_exp = lax.axis_size("expert")
    tokens, hidden_all = hidden.shape[2:]
    features = out_grad.shape[3]
    slices = changed.shape[3]
    rows = first_moment.shape[0]
    slice_rows = rows // slices
    chunks = features // LANES
    flat = (rows * chunks, LANES)
    f32, bf16 = jnp.float32, jnp.bfloat16
    any_spec = pl.BlockSpec(memory_space=pltpu.HBM)
    vmem = pl.BlockSpec(memory_space=pltpu.VMEM)
    dma = pltpu.SemaphoreType.DMA
    regular = pltpu.SemaphoreType.REGULAR
    swapped = jnp.swapaxes(placement, 3, 4)
    results = pl.pallas_call(
        functools.partial(kernel, n_dp, n_exp, slices),
        out_shape=(
            pltpu.VMEM(flat, f32),
            pltpu.VMEM(flat, f32),
            pltpu.VMEM((n_exp, chunks, SLOTS, slice_rows, LANES), bf16),
        ),
        in_specs=[any_spec] * 3 + [pl.BlockSpec(memory_space=pltpu.SMEM)] + [any_spec] * 4,
        out_specs=(vmem, vmem, vmem),
        scratch_shapes=[
            pltpu.SMEM(block_list.shape, jnp.int32),
            pltpu.SMEM(changed.shape, jnp.int32),
            pltpu.SMEM(swapped.shape, jnp.int32),
            pltpu.VMEM((tokens, hidden_all), bf16),
            pltpu.VMEM((tokens, features), bf16),
            pltpu.VMEM((hidden_all, tokens), bf16),
            pltpu.VMEM(flat, f32),
            pltpu.VMEM(flat, f32),
            pltpu.VMEM((rows, LANES), jnp.int32),
            pltpu.VMEM((chunks, 2, n_dp // 2, rows, LANES), bf16),
            pltpu.VMEM((chunks, n_dp // 2, rows, LANES), bf16),
            pltpu.VMEM((chunks, n_dp // 2, rows, LANES), bf16),
            pltpu.VMEM((slices + 1, slice_rows, LANES), bf16),
            pltpu.VMEM((n_exp, chunks, SLOTS, slice_rows, LANES), bf16),
            pltpu.VMEM((8, LANES), jnp.int32),
            pltpu.SMEM((8, LANES), jnp.int32),
            dma((3 + hidden_all // 512,)),
            dma((3,)),
            dma(()),
            dma((chunks,)),
            dma((chunks,)),
            dma((chunks, n_dp // 2)),
            dma((chunks, n_dp // 2)),
            dma((3, n_exp)),
            dma((3, n_exp)),
            regular((n_exp,)),
        ],
        compiler_params=pltpu.CompilerParams(
            collective_id=0, has_side_effects=True, vmem_limit_bytes=32 << 20
        ),
    )(
        in_hbm(hidden),
        in_hbm(out_grad),
        in_hbm(block_list),
        block_count,
        in_hbm(first_moment.reshape(flat)),
        in_hbm(second_moment.reshape(flat)),
        in_hbm(changed),
        in_hbm(swapped),
    )
    first_next, second_next, inbox = pl.pallas_call(
        store_kernel,
        out_shape=(
            jax.ShapeDtypeStruct(flat, f32),
            jax.ShapeDtypeStruct(flat, f32),
            jax.ShapeDtypeStruct((n_exp, SLOTS, slice_rows, features), bf16),
        ),
        in_specs=[vmem] * 3,
        out_specs=(any_spec,) * 3,
        scratch_shapes=[dma((2 + chunks,))],
    )(*(pltpu.with_memory_space_constraint(x, pltpu.VMEM) for x in results))
    shape = first_moment.shape
    return (
        first_next.reshape(shape),
        second_next.reshape(shape),
        inbox[None, None, None],
    )


def solution(mesh):
    return jax.shard_map(
        on_device,
        mesh=mesh,
        in_specs=(
            P("dp", "expert", None, None),
            P("dp", "expert", None, "tensor"),
            P("dp", "expert", None),
            P("dp", "expert"),
            P("dp", "expert", "tensor"),
            P("dp", "expert", "tensor"),
            P("dp", "expert", "tensor", None),
            P("dp", "expert", "tensor", None, None),
        ),
        out_specs=(
            P("dp", "expert", "tensor"),
            P("dp", "expert", "tensor"),
            P("dp", "expert", "tensor", None, None, None, None),
        ),
        check_vma=False,
    )
```

```python
import functools

import jax
import jax.numpy as jnp
from jax import lax
from jax.experimental import pallas as pl
from jax.experimental.pallas import tpu as pltpu
from jax.sharding import PartitionSpec as P

MESH = pl.DeviceIdType.MESH
BLOCK = 128
LANES = 128
SLOTS = 2

beta_one = 0.9
beta_two = 0.95
adam_eps = 1e-08
step_number = 50.0


def kernel(
    n_dp,
    n_exp,
    slices,
    hidden,
    out_grad,
    block_list_hbm,
    block_count,
    first,
    second,
    changed_hbm,
    placement_hbm,
    first_out,
    second_out,
    pack_in,
    block_list,
    changed,
    placement,
    h_buf,
    g_buf,
    ht_buf,
    m_buf,
    v_buf,
    keep_buf,
    part,
    pair_in,
    part_in,
    upd,
    pack,
    idx_vec,
    idx,
    load_sem,
    small_sem,
    idx_sem,
    pair_send,
    pair_recv,
    rs_send,
    rs_recv,
    z_send,
    z_recv,
    ready,
):
    dp = lax.axis_index("dp")
    me = lax.axis_index("expert")
    pairs = n_dp // 2
    place = dp // 2
    side = dp - 2 * place
    sibling = 2 * place + 1 - side
    tokens, hidden_all = h_buf.shape
    rows = hidden_all // n_dp
    slice_rows = rows // slices
    chunks = g_buf.shape[1] // LANES
    blocks = tokens // BLOCK

    barrier = pltpu.get_barrier_semaphore()
    for peer in [sibling] + [2 * lax.rem(place + off, pairs) + side for off in range(1, pairs)]:
        pl.semaphore_signal(barrier, inc=1, device_id={"dp": peer}, device_id_type=MESH)

    @pl.when(me == 0)
    def _():
        pl.semaphore_signal(barrier, inc=1, device_id={"expert": 1}, device_id_type=MESH)

    @pl.when(me > 0)
    def _():
        @pl.loop(1, n_exp)
        def _(off):
            @pl.when(me + off < n_exp)
            def _():
                pl.semaphore_signal(
                    barrier, inc=1, device_id={"expert": me + off}, device_id_type=MESH
                )

    small = [
        pltpu.make_async_copy(src, dst, small_sem.at[i])
        for i, (src, dst) in enumerate(
            (
                (changed_hbm, changed),
                (placement_hbm, placement),
                (block_list_hbm, block_list),
            )
        )
    ]
    for cp in small:
        cp.start()
    groups = hidden_all // 512
    loads = [pltpu.make_async_copy(out_grad.at[0, 0], g_buf, load_sem.at[0])]
    for i in range(groups):
        cols = pl.ds(i * 512, 512)
        loads.append(
            pltpu.make_async_copy(hidden.at[0, 0, :, cols], h_buf.at[:, cols], load_sem.at[1 + i])
        )
    loads.append(pltpu.make_async_copy(first, m_buf, load_sem.at[1 + groups]))
    loads.append(pltpu.make_async_copy(second, v_buf, load_sem.at[2 + groups]))
    for cp in loads[: 1 + groups]:
        cp.start()

    for cp in small:
        cp.wait()
    loads[0].wait()
    for b in range(blocks):
        live = jnp.int32(0)
        for j in range(blocks):
            hit = (block_list[0, 0, j] == b) & (block_count[0, 0] > j)
            live = live | hit.astype(jnp.int32)
        at = pl.ds(b * BLOCK, BLOCK)
        block = g_buf[at, :]
        g_buf[at, :] = jnp.where(live > 0, block, jnp.zeros_like(block))
    for i in range(groups):
        loads[1 + i].wait()
        for j in range(512 // LANES):
            at = i * 512 + j * LANES
            ht_buf[pl.ds(at, LANES), :] = h_buf[:, pl.ds(at, LANES)].T

    def pair_copy(c):
        return pltpu.make_async_remote_copy(
            src_ref=part.at[c, 1 - side],
            dst_ref=pair_in.at[c],
            send_sem=pair_send.at[c],
            recv_sem=pair_recv.at[c],
            device_id={"dp": sibling},
            device_id_type=MESH,
        )

    def reduce_copy(c, peer, slot):
        return pltpu.make_async_remote_copy(
            src_ref=part.at[c, side, peer],
            dst_ref=part_in.at[c, slot],
            send_sem=rs_send.at[c, peer],
            recv_sem=rs_recv.at[c, slot],
            device_id={"dp": 2 * peer + side},
            device_id_type=MESH,
        )

    def tell(who, peer):
        pl.semaphore_signal(
            ready.at[who], inc=1, device_id={"expert": peer}, device_id_type=MESH
        )

    def enter():
        pl.semaphore_wait(barrier, pairs + jnp.where(me == 1, 1, jnp.maximum(me - 1, 0)))

        @pl.loop(0, n_exp - 1)
        def _(peer):
            @pl.when((peer < me) & ((peer > 0) | (me == 1)))
            def _():
                tell(me, peer)

    def multiply(c):
        width = 2 * LANES
        for d in range(n_dp):
            prod = jnp.dot(
                ht_buf[pl.ds(d * rows, rows), :],
                g_buf[:, pl.ds(c * LANES, width)],
                preferred_element_type=jnp.float32,
            ).astype(part.dtype)
            part[c, d % 2, d // 2] = prod[:, :LANES]
            part[c + 1, d % 2, d // 2] = prod[:, LANES:]
        if c == 0:
            enter()
        pair_copy(c).start()
        pair_copy(c + 1).start()

    def add_pair(c):
        pair_copy(c).wait_recv()
        mine = part[c, side].astype(jnp.float32) + pair_in[c].astype(jnp.float32)
        part[c, side] = mine.astype(part.dtype)
        for off in (2, 1, 3):
            reduce_copy(c, lax.rem(place + off, pairs), place).start()

    multiply(0)
    for cp in loads[1 + groups :]:
        cp.start()

    lane = lax.broadcasted_iota(jnp.int32, (8, LANES), 1)
    owner_of = lane // SLOTS
    slot_of = lane - owner_of * SLOTS
    count = jnp.zeros((8, LANES), jnp.int32)
    table = jnp.full((8, LANES), slices, jnp.int32)
    for s in range(slices):
        value = jnp.where(changed[0, 0, 0, s] > 0, s, slices)
        for k in range(2):
            hit = owner_of == placement[0, 0, 0, k, s]
            table = jnp.where(hit & (count == slot_of), value, table)
            count = count + hit.astype(jnp.int32)
    idx_vec[...] = table
    idx_copy = pltpu.make_async_copy(idx_vec, idx, idx_sem)
    idx_copy.start()
    for s in range(slices):
        keep_buf[pl.ds(s * slice_rows, slice_rows), :] = jnp.full(
            (slice_rows, LANES), changed[0, 0, 0, s], jnp.int32
        )
    upd[slices] = jnp.zeros(upd.shape[1:], upd.dtype)

    add_pair(0)
    multiply(2)
    add_pair(1)

    loads[1 + groups].wait()
    loads[2 + groups].wait()
    idx_copy.wait()

    phases = ((0, 1), (1, chunks - 1), (0, chunks))
    middle = 5 * n_exp // 8

    def route_copy(p, peer, slot):
        at = pl.ds(*phases[p])
        return pltpu.make_async_remote_copy(
            src_ref=pack.at[peer, at],
            dst_ref=pack_in.at[slot, at],
            send_sem=z_send.at[p, peer],
            recv_sem=z_recv.at[p, slot],
            device_id={"expert": peer},
            device_id_type=MESH,
        )

    def far_first(low, high, act):
        @pl.loop(0, high - low)
        def _(i):
            act(high - 1 - i)

    def send_left(p):
        def act(off):
            @pl.when(me - off > 0)
            def _():
                route_copy(p, me - off, me).start()

        return act

    def send_right(p):
        def act(off):
            @pl.when(me + off < n_exp)
            def _():
                if p != 1:

                    pl.semaphore_wait(ready.at[me + off], 1)

                    @pl.when(me == 1)
                    def _():
                        tell(0, me + off)

                route_copy(p, me + off, me).start()

        return act

    def wait_sent(p):
        def act(off):
            @pl.when(me - off > 0)
            def _():
                route_copy(p, me - off, me).wait_send()

            @pl.when(me + off < n_exp)
            def _():
                route_copy(p, me + off, me).wait_send()

        return act

    def wait_received(p):
        def act(off):
            @pl.when(me - off >= 0)
            def _():
                route_copy(p, me - off, me - off).wait_recv()

            @pl.when((me > 0) & (me + off < n_exp))
            def _():
                route_copy(p, me + off, me + off).wait_recv()

        return act

    corr_one = 1.0 - beta_one**step_number
    corr_two = 1.0 - beta_two**step_number
    for c in range(chunks):
        total = part[c, side, place].astype(jnp.float32)
        for off in range(1, pairs):
            peer = lax.rem(place + off, pairs)
            reduce_copy(c, peer, peer).wait_recv()
            total = total + part_in[c, peer].astype(jnp.float32)
        if c == 0:
            add_pair(2)
            add_pair(3)
        at = pl.ds(c, rows, stride=chunks)
        m_old = m_buf[at, :]
        v_old = v_buf[at, :]
        keep = keep_buf[...] > 0
        m_next = beta_one * m_old + (1.0 - beta_one) * total
        v_next = beta_two * v_old + (1.0 - beta_two) * total * total
        update = m_next / corr_one / (jnp.sqrt(v_next / corr_two) + adam_eps)
        first_out[at, :] = jnp.where(keep, m_next, m_old)
        second_out[at, :] = jnp.where(keep, v_next, v_old)
        upd[pl.ds(0, slices)] = update.astype(upd.dtype).reshape(slices, slice_rows, LANES)
        for n in range(n_exp * SLOTS):
            pack[n // SLOTS, c, n % SLOTS] = upd[idx[0, n]]
        if c == 0:
            far_first(1, middle + 1, send_left(0))
            pl.loop(1, middle + 1)(send_right(0))

    far_first(middle + 1, n_exp, send_left(2))
    @pl.when(me > 1)
    def _():
        pl.semaphore_wait(ready.at[0], 1)
        tell(me, 0)

    @pl.when(me > 0)
    def _():
        route_copy(2, 0, me).start()

    far_first(1, middle + 1, send_left(1))
    pl.loop(middle + 1, n_exp)(send_right(2))
    far_first(1, middle + 1, send_right(1))

    pack_in[me] = pack[me]
    for c in range(chunks):
        pair_copy(c).wait_send()
        for off in range(1, pairs):
            reduce_copy(c, lax.rem(place + off, pairs), place).wait_send()
    far_first(1, middle + 1, wait_sent(0))
    far_first(1, middle + 1, wait_sent(1))
    far_first(middle + 1, n_exp, wait_sent(2))
    far_first(1, middle + 1, wait_received(0))
    far_first(middle + 1, n_exp, wait_received(2))
    far_first(1, middle + 1, wait_received(1))

    @pl.when(me > 0)
    def _():
        route_copy(2, 0, me).wait_send()

    @pl.when(me == 0)
    def _():
        @pl.loop(1, n_exp)
        def _(peer):
            route_copy(2, peer, peer).wait_recv()


def store_kernel(first, second, pack, first_out, second_out, inbox, sem):
    chunks = pack.shape[1]
    copies = [
        pltpu.make_async_copy(first, first_out, sem.at[0]),
        pltpu.make_async_copy(second, second_out, sem.at[1]),
    ]
    for c in range(chunks):
        copies.append(
            pltpu.make_async_copy(
                pack.at[:, c], inbox.at[:, :, :, pl.ds(c * LANES, LANES)], sem.at[2 + c]
            )
        )
    for cp in copies:
        cp.start()
    for cp in copies:
        cp.wait()


def in_hbm(x):
    return pltpu.with_memory_space_constraint(x, pltpu.HBM)


def on_device(
    hidden, out_grad, block_list, block_count, first_moment, second_moment, changed, placement
):
    n_dp = lax.axis_size("dp")
    n_exp = lax.axis_size("expert")
    tokens, hidden_all = hidden.shape[2:]
    features = out_grad.shape[3]
    slices = changed.shape[3]
    rows = first_moment.shape[0]
    slice_rows = rows // slices
    chunks = features // LANES
    flat = (rows * chunks, LANES)
    f32, bf16 = jnp.float32, jnp.bfloat16
    any_spec = pl.BlockSpec(memory_space=pltpu.HBM)
    vmem = pl.BlockSpec(memory_space=pltpu.VMEM)
    dma = pltpu.SemaphoreType.DMA
    regular = pltpu.SemaphoreType.REGULAR
    swapped = jnp.swapaxes(placement, 3, 4)
    results = pl.pallas_call(
        functools.partial(kernel, n_dp, n_exp, slices),
        out_shape=(
            pltpu.VMEM(flat, f32),
            pltpu.VMEM(flat, f32),
            pltpu.VMEM((n_exp, chunks, SLOTS, slice_rows, LANES), bf16),
        ),
        in_specs=[any_spec] * 3 + [pl.BlockSpec(memory_space=pltpu.SMEM)] + [any_spec] * 4,
        out_specs=(vmem, vmem, vmem),
        scratch_shapes=[
            pltpu.SMEM(block_list.shape, jnp.int32),
            pltpu.SMEM(changed.shape, jnp.int32),
            pltpu.SMEM(swapped.shape, jnp.int32),
            pltpu.VMEM((tokens, hidden_all), bf16),
            pltpu.VMEM((tokens, features), bf16),
            pltpu.VMEM((hidden_all, tokens), bf16),
            pltpu.VMEM(flat, f32),
            pltpu.VMEM(flat, f32),
            pltpu.VMEM((rows, LANES), jnp.int32),
            pltpu.VMEM((chunks, 2, n_dp // 2, rows, LANES), bf16),
            pltpu.VMEM((chunks, n_dp // 2, rows, LANES), bf16),
            pltpu.VMEM((chunks, n_dp // 2, rows, LANES), bf16),
            pltpu.VMEM((slices + 1, slice_rows, LANES), bf16),
            pltpu.VMEM((n_exp, chunks, SLOTS, slice_rows, LANES), bf16),
            pltpu.VMEM((8, LANES), jnp.int32),
            pltpu.SMEM((8, LANES), jnp.int32),
            dma((3 + hidden_all // 512,)),
            dma((3,)),
            dma(()),
            dma((chunks,)),
            dma((chunks,)),
            dma((chunks, n_dp // 2)),
            dma((chunks, n_dp // 2)),
            dma((3, n_exp)),
            dma((3, n_exp)),
            regular((n_exp,)),
        ],
        compiler_params=pltpu.CompilerParams(
            collective_id=0, has_side_effects=True, vmem_limit_bytes=32 << 20
        ),
    )(
        in_hbm(hidden),
        in_hbm(out_grad),
        in_hbm(block_list),
        block_count,
        in_hbm(first_moment.reshape(flat)),
        in_hbm(second_moment.reshape(flat)),
        in_hbm(changed),
        in_hbm(swapped),
    )
    first_next, second_next, inbox = pl.pallas_call(
        store_kernel,
        out_shape=(
            jax.ShapeDtypeStruct(flat, f32),
            jax.ShapeDtypeStruct(flat, f32),
            jax.ShapeDtypeStruct((n_exp, SLOTS, slice_rows, features), bf16),
        ),
        in_specs=[vmem] * 3,
        out_specs=(any_spec,) * 3,
        scratch_shapes=[dma((2 + chunks,))],
    )(*(pltpu.with_memory_space_constraint(x, pltpu.VMEM) for x in results))
    shape = first_moment.shape
    return (
        first_next.reshape(shape),
        second_next.reshape(shape),
        inbox[None, None, None],
    )


def solution(mesh):
    return jax.shard_map(
        on_device,
        mesh=mesh,
        in_specs=(
            P("dp", "expert", None, None),
            P("dp", "expert", None, "tensor"),
            P("dp", "expert", None),
            P("dp", "expert"),
            P("dp", "expert", "tensor"),
            P("dp", "expert", "tensor"),
            P("dp", "expert", "tensor", None),
            P("dp", "expert", "tensor", None, None),
        ),
        out_specs=(
            P("dp", "expert", "tensor"),
            P("dp", "expert", "tensor"),
            P("dp", "expert", "tensor", None, None, None, None),
        ),
        check_vma=False,
    )
```
